256 devices in a mesh: cont: 8 (over y, core), dev: 32 (over x, z).
Axes of the slice: x: 4, y: 4, z: 8, core: 2. Of those that a mesh axis runs over, the one named last changes fastest.
Arguments:
- station_values: bfloat16 [256, 128, 366], P(('cont', 'dev')), may hold values from -6 to 6
- krige_weights: bfloat16 [256, 128, 512], P(('cont', 'dev')), may hold values from -0.25 to 0.25
- inv_factor: bfloat16 [256, 128, 128], P(('cont', 'dev')), may hold values from -4 to 4
- cond_blocks: int32 [256, 4], P(('cont', 'dev')), may hold values from 0 to 255, as said below
- station_xy: bfloat16 [256, 2, 128], P(('cont', 'dev')), may hold values from 0 to 2
- cell_xy: float32 [2, 1048576], P(None, ('cont', 'dev')), may hold values from 0 to 2
- tile_blocks: int32 [1024, 16], P(('cont', 'dev')), may hold values from 0 to 255, as said below
- rain: float32 [60, 1048576], P(None, ('cont', 'dev')), may hold values from -6 to 6
Outputs:
- thresholds: bfloat16 [1048576, 366], P(('cont', 'dev'))
- exceed_share: float32 [1048576], P(('cont', 'dev'))
The draws below stay inside these ranges and needn't reach their ends.
Inputs may be any that keep to these rules, and one draw needn't show every extreme that they name: `cond_blocks`: row b names 4 different blocks of b's continent c (blocks c * 32 to c * 32 + 31), never b itself. `tile_blocks`: row t names 16 different blocks, each of the continent of tile t or of the continent before it (continent c - 1, and 7 before 0); tile t lies in continent t // 128.
All inputs are finite; a program needn't handle non-finite values.
Results may differ from the reference program's by a relative error of at most 0.0069.
Values may be sent and summed in bfloat16 or wider, within the bound.
A program may use at most 64 MiB of HBM per device.

```python
import jax
import jax.numpy as jnp
from jax import lax

BS = 128
NCOND = 4
DAYS = 366
S = 16
TILE = 1024
TILES_DEV = 4
WIN = 60
WSTART = 150
BLK_CONT = 32
CONTS = 8
NB = 256
NTILES = 1024
NCELLS = 1048576


def draw_inv_factor(key, part):
    key = jax.random.fold_in(key, 13)
    diag_key, off_key = jax.random.split(key)
    diagonal = jax.random.uniform(diag_key, (NB, BS, 1), jnp.float32, 0.5, 2.0)
    off_part = jnp.clip(jax.random.normal(off_key, (NB, BS, BS), jnp.float32), -5.0, 5.0) * (0.6 / BS ** 0.5)
    eye_part = jnp.eye(BS, dtype=jnp.float32)[None, :, :]
    return (off_part + diagonal * eye_part).astype(jnp.bfloat16)


def draw_cond_blocks(key, part):
    key = jax.random.fold_in(key, 11)
    scores = jax.random.randint(key, (NB, BLK_CONT - 1), 0, 1 << 20) * (BLK_CONT - 1) + jnp.arange(BLK_CONT - 1, dtype=jnp.int32)[None, :]
    offsets = jnp.argsort(scores, axis=1)[:, :NCOND].astype(jnp.int32) + 1
    block_index = jnp.arange(NB, dtype=jnp.int32)
    continent = block_index // BLK_CONT
    local_index = block_index % BLK_CONT
    return (continent[:, None] * BLK_CONT + (local_index[:, None] + offsets) % BLK_CONT).astype(jnp.int32)


def draw_tile_blocks(key, part):
    key = jax.random.fold_in(key, 17)
    scores = jax.random.randint(key, (NTILES, 2 * BLK_CONT), 0, 1 << 20) * (2 * BLK_CONT) + jnp.arange(2 * BLK_CONT, dtype=jnp.int32)[None, :]
    picked = jnp.argsort(scores, axis=1)[:, :S].astype(jnp.int32)
    tile_index = jnp.arange(NTILES, dtype=jnp.int32)
    continent = (tile_index // (TILES_DEV * BLK_CONT))[:, None]
    previous = (continent + CONTS - 1) % CONTS
    return jnp.where(picked < BLK_CONT, previous * BLK_CONT + picked, continent * BLK_CONT + picked - BLK_CONT).astype(jnp.int32)


def shard_levels(stream_key, extent, cuts, smallest, high):
    def one(position, shards_of):
        draws = jax.random.uniform(jax.random.fold_in(jax.random.fold_in(stream_key, 6), position), (shards_of,), jnp.float32, smallest / len(cuts), high / len(cuts))
        return jnp.repeat(jnp.exp(draws), extent[position] // shards_of).reshape((-1,) + (1,) * (len(extent) - position - 1))

    loudness = one(*cuts[0])
    for cut in cuts[1:]:
        loudness = loudness * one(*cut)
    return loudness


def scatter_about(key, extent, deviation, reach, cuts=(), held_as=jnp.bfloat16):
    values = deviation * jax.random.normal(key, extent, jnp.float32)
    if cuts:
        values = values * shard_levels(key, extent, cuts, -0.22, 0.18)
    return jnp.clip(values, -reach, reach).astype(held_as)


def setup_inputs(seed: int = 0) -> dict:
    seeds = jax.random.split(jax.random.key(seed), 9)
    station_values = scatter_about(seeds[0], (NB, BS, DAYS), 1.0, 6.0, ((0, 256),))
    krige_weights = scatter_about(seeds[1], (NB, BS, NCOND * BS), (NCOND * BS) ** -0.5, 0.25, ((0, 256),))
    inv_factor = draw_inv_factor(jax.random.fold_in(seeds[8], 71), 0)
    cond_blocks = draw_cond_blocks(jax.random.fold_in(seeds[8], 71), 0)
    station_xy = jnp.clip(2.0 * jax.random.uniform(seeds[4], (NB, 2, BS), jnp.float32) ** shard_levels(seeds[4], (NB, 2, BS), ((0, 256),), -0.2, 0.2), 0.0, 2.0).astype(jnp.bfloat16)
    cell_xy = jnp.clip(2.0 * jax.random.uniform(seeds[5], (2, NCELLS), jnp.float32) ** shard_levels(seeds[5], (2, NCELLS), ((1, 256),), -0.2, 0.2), 0.0, 2.0)
    tile_blocks = draw_tile_blocks(jax.random.fold_in(seeds[8], 71), 0)
    rain = scatter_about(seeds[7], (WIN, NCELLS), 1.0, 6.0, ((1, 256),), jnp.float32)
    return {"station_values": station_values, "krige_weights": krige_weights, "inv_factor": inv_factor, "cond_blocks": cond_blocks, "station_xy": station_xy, "cell_xy": cell_xy, "tile_blocks": tile_blocks, "rain": rain}


sharpness = 4.0
cov_scale = 0.0625

def covariance(cell_x, cell_y, station_x, station_y, length):
    distance_sq = (cell_x[:, None] - station_x[None, :]) ** 2 + (cell_y[:, None] - station_y[None, :]) ** 2
    return (jnp.exp(-jnp.sqrt(distance_sq + (length * 0.1) ** 2) / length) * cov_scale).astype(jnp.bfloat16)

def exceedance(threshold, rain_tile):
    window = jnp.roll(threshold, -WSTART, axis=1)[:, :WIN]
    return lax.optimization_barrier(jnp.mean(jax.nn.sigmoid((rain_tile.T - window) * sharpness), axis=1))

def whiten_block(values_block, prior_rows, weights_block, factor_block):
    predicted = jnp.dot(weights_block, prior_rows, preferred_element_type=jnp.float32)
    innovation = (values_block.astype(jnp.float32) - predicted).astype(jnp.bfloat16)
    whitened = jnp.dot(factor_block, innovation, preferred_element_type=jnp.float32).astype(jnp.bfloat16)
    return lax.dot_general(factor_block, whitened, (((0,), (0,)), ((), ())), preferred_element_type=jnp.float32).astype(jnp.bfloat16)

def reference(station_values, krige_weights, inv_factor, cond_blocks, station_xy, cell_xy, tile_blocks, rain):

    def one_block(block_index):
        prior_rows = jnp.take(station_values, cond_blocks[block_index], axis=0).reshape(NCOND * BS, DAYS)
        return whiten_block(station_values[block_index], prior_rows, krige_weights[block_index], inv_factor[block_index])
    kweights = lax.map(one_block, jnp.arange(NB, dtype=jnp.int32))
    length = 9.0 * (S * BS) ** (-0.5)

    def one_tile(tile_index):
        tile_ids = tile_blocks[tile_index]
        chosen = jnp.take(kweights, tile_ids, axis=0).reshape(S * BS, DAYS)
        coords = jnp.take(station_xy, tile_ids, axis=0).astype(jnp.float32)
        station_x = coords[:, 0, :].reshape(S * BS)
        station_y = coords[:, 1, :].reshape(S * BS)
        cell_coords = lax.dynamic_slice_in_dim(cell_xy, tile_index * TILE, TILE, 1)
        weights_tile = covariance(cell_coords[0], cell_coords[1], station_x, station_y, length)
        threshold = jnp.dot(weights_tile, chosen, preferred_element_type=jnp.float32)
        rain_tile = lax.dynamic_slice_in_dim(rain, tile_index * TILE, TILE, 1)
        return (threshold.astype(jnp.bfloat16), exceedance(threshold, rain_tile))
    threshold_all, share_all = lax.map(one_tile, jnp.arange(NTILES, dtype=jnp.int32))
    return (threshold_all.reshape(NCELLS, DAYS), share_all.reshape(NCELLS))
```

```python
import functools
import math

import jax
import jax.numpy as jnp
from jax import lax
from jax.experimental import pallas as pl
from jax.experimental.pallas import tpu as pltpu
from jax.sharding import PartitionSpec as P

MESH = pl.DeviceIdType.MESH
BF16 = jnp.bfloat16
F32 = jnp.float32

XS, ZS = 4, 8
GROUP = XS * ZS
CONTS = 8
BS = 128
HALF = 64
QUARTER = 32
DAYS = 366
COLS = 384
NCOND = 4
LISTED = 16
STATIONS = LISTED * BS
TILES = 4
TILE = 1024
CELLS = TILES * TILE
WIN = 60
WSTART = 150
WLANE = WSTART // 128 * 128
WROW = (WSTART - WLANE) // 8 * 8
WOFF = WSTART - WLANE - WROW
WROWS = -(-(WOFF + WIN) // 8) * 8
LENGTH = 9.0 * STATIONS**-0.5
SCALE = math.log2(math.e) / LENGTH
NUGGET = (LENGTH * 0.1 * SCALE) ** 2
CHUNK = 512


class Place:
    def __init__(self):
        dev = lax.axis_index("dev")
        cont = lax.axis_index("cont")
        self.dev, self.cont = dev, cont
        self.x, self.z = dev // ZS, dev % ZS
        self.xs = [self.x, self.at_x(-1), self.at_x(1), self.at_x(2)]
        self.zs = [self.z] + [self.at_z(d) for s in (1, 2, 3) for d in (-s, s)] + [self.at_z(4)]
        self.xl, self.xr = self.xs[1] * ZS + self.z, self.xs[2] * ZS + self.z
        self.zl, self.zr = self.x * ZS + self.zs[1], self.x * ZS + self.zs[2]
        self.ahead = lax.rem(cont + 1, CONTS)
        self.behind = lax.rem(cont + CONTS - 1, CONTS)
        self.even = lax.rem(cont, 2) == 0

    def at_x(self, step):
        return lax.rem(self.x + (step + XS), XS)

    def at_z(self, step):
        return lax.rem(self.z + (step + ZS), ZS)


def remote(src, dst, send, recv, **device):
    return pltpu.make_async_remote_copy(
        src_ref=src, dst_ref=dst, send_sem=send, recv_sem=recv, device_id=device, device_id_type=MESH
    )


class Gather:
    def __init__(self, place, buf, send, recv):
        self.p, self.buf, self.send, self.recv = place, buf, send, recv

    def push(self, slot, sem, dev, rows=None):
        ref = self.buf.at[slot] if rows is None else self.buf.at[slot, pl.ds(rows, QUARTER)]
        remote(ref, ref, self.send, self.recv.at[sem], dev=dev).start()

    def arrived(self, slot, sem, rows=None):
        ref = self.buf.at[slot] if rows is None else self.buf.at[slot, pl.ds(rows, QUARTER)]
        remote(ref, ref, self.send, self.recv.at[sem], dev=self.p.dev).wait_recv()

    def sent(self):
        ref = self.buf.at[pl.ds(0, GROUP - 1)]
        remote(ref, ref, self.send, self.recv.at[0], dev=self.p.dev).wait_send()


class GatherA(Gather):
    def slot(self, z, x):
        return z * XS + x

    def zsem(self, s, way, j):
        return 4 + ((s - 1) * 2 + way) * XS + j

    def spread_z(self, j):
        p = self.p
        slot = self.slot(p.z, p.xs[j])
        self.push(slot, self.zsem(1, 0, j), p.zr)
        self.push(slot, self.zsem(1, 1, j), p.zl)

    def start(self):
        p = self.p
        own = self.slot(p.z, p.x)
        self.push(own, 0, p.xr)
        self.push(own, 1, p.xl)
        self.spread_z(0)

    def round(self, r):
        p = self.p
        if r == 1:
            left, right = self.slot(p.z, p.xs[1]), self.slot(p.z, p.xs[2])
            self.arrived(left, 0)
            self.push(left, 2, p.xr, 0)
            self.spread_z(1)
            self.arrived(right, 1)
            self.push(right, 3, p.xl, QUARTER)
            self.spread_z(2)
        if r == 2:
            far = self.slot(p.z, p.xs[3])
            self.arrived(far, 2, 0)
            self.arrived(far, 3, QUARTER)
            self.spread_z(3)
        for j, hop in enumerate((0, 1, 1, 2)):
            s = r - hop
            if 1 <= s <= 3:
                left, right = self.slot(p.at_z(-s), p.xs[j]), self.slot(p.at_z(s), p.xs[j])
                self.arrived(left, self.zsem(s, 0, j))
                if s < 3 or j % 2 == 0:
                    self.push(left, self.zsem(s + 1, 0, j), p.zr)
                self.arrived(right, self.zsem(s, 1, j))
                if s < 3 or j % 2 == 1:
                    self.push(right, self.zsem(s + 1, 1, j), p.zl)
            if s == 4:
                self.arrived(self.slot(p.at_z(4), p.xs[j]), self.zsem(4, j % 2, j))


A_SEMS = 4 + 4 * 2 * XS


class GatherB(Gather):
    def slot(self, x, z):
        return x * ZS + z

    def spread_x(self, i):
        p = self.p
        slot = self.slot(p.x, p.zs[i])
        self.push(slot, 8 + i, p.xr)
        self.push(slot, 16 + i, p.xl)

    def start(self):
        p = self.p
        own = self.slot(p.x, p.z)
        self.push(own, 0, p.zr)
        self.push(own, 1, p.zl)
        self.spread_x(0)

    def pass_x(self, i):
        p = self.p
        left, right = self.slot(p.xs[1], p.zs[i]), self.slot(p.xs[2], p.zs[i])
        self.arrived(left, 8 + i)
        if i in (0, 7):
            self.push(left, 24 + i, p.xr, 0)
        elif i % 2:
            self.push(left, 24 + i, p.xr)
        self.arrived(right, 16 + i)
        if i in (0, 7):
            self.push(right, 32 + i, p.xl, QUARTER)
        elif i % 2 == 0:
            self.push(right, 32 + i, p.xl)

    def end_x(self, i):
        p = self.p
        far = self.slot(p.xs[3], p.zs[i])
        if i in (0, 7):
            self.arrived(far, 24 + i, 0)
            self.arrived(far, 32 + i, QUARTER)
        elif i % 2:
            self.arrived(far, 24 + i)
        else:
            self.arrived(far, 32 + i)

    def round(self, r):
        p = self.p
        if 1 <= r <= 3:
            left, right = self.slot(p.x, p.at_z(-r)), self.slot(p.x, p.at_z(r))
            self.arrived(left, 2 * r - 2)
            self.push(left, 2 * r, p.zr, 0 if r == 3 else None)
            self.spread_x(2 * r - 1)
            self.arrived(right, 2 * r - 1)
            self.push(right, 2 * r + 1, p.zl, QUARTER if r == 3 else None)
            self.spread_x(2 * r)
        if r == 4:
            far = self.slot(p.x, p.zs[7])
            self.arrived(far, 6, 0)
            self.arrived(far, 7, QUARTER)
            self.spread_x(7)
        for s, members in enumerate(((0,), (1, 2), (3, 4), (5, 6), (7,))):
            for i in members:
                if r == s + 1:
                    self.pass_x(i)
                if r == s + 2:
                    self.end_x(i)


B_SEMS = 40


def dot(a, b, dims=((1,), (0,))):
    return lax.dot_general(a, b, (dims, ((), ())), preferred_element_type=F32)


def kernel(
    cond, tiles, sv, weights, factor, xy, cells, rain,
    out, share,
    sva, svb, kwa, kwb, coords, cellx, celly, rain_raw, rain_win, prior, cov, chosen,
    rain_sem,
    c_send, c_recv, cz_send, cc_send,
    sa_send, sa_recv, sb_send, sb_recv,
    ka_send, ka_recv, kb_send, kb_recv, kp_send, kp_recv,
    fa_send, fa_recv, fb_send, fb_recv, inj_send, inj_recv,
):
    p = Place()
    rain_copy = pltpu.make_async_copy(rain, rain_raw, rain_sem)
    rain_copy.start()

    ga = GatherA(p, sva, sa_send, sa_recv)
    gb = GatherB(p, svb, sb_send, sb_recv)
    slot_a, slot_b = ga.slot(p.z, p.x), gb.slot(p.x, p.z)

    barrier = pltpu.get_barrier_semaphore()
    x_peers = [p.at_x(s) * ZS + p.z for s in (1, 2, 3)]
    z_peers = [p.x * ZS + p.at_z(s) for s in range(1, ZS)]
    for peer in x_peers + z_peers:
        pl.semaphore_signal(barrier, inc=1, device_id={"dev": peer}, device_id_type=MESH)
    pl.semaphore_signal(barrier, inc=1, device_id={"cont": p.behind}, device_id_type=MESH)

    tail = jnp.zeros((HALF, COLS - DAYS), BF16)
    sva[slot_a] = jnp.concatenate([sv[0, :HALF, :], tail], axis=1)
    svb[slot_b] = jnp.concatenate([sv[0, HALF:, :], tail], axis=1)
    coords[1, slot_a] = jnp.concatenate(
        [xy[0].astype(F32) * SCALE, jnp.zeros((6, BS), F32)], axis=0
    )
    pl.semaphore_wait(barrier, XS + ZS - 1)

    def coord_x(s):
        ref = coords.at[1, slot_a]
        return remote(ref, ref, c_send, c_recv.at[s], dev=x_peers[s - 1])

    for s in (1, 2, 3):
        coord_x(s).start()
    ga.start()
    gb.start()

    def place_cells(first, last):
        def one(c, carry):
            lanes = pl.ds(pl.multiple_of(c * 128, 128), 128)
            for row, held in ((0, cellx), (1, celly)):
                line = cells[row : row + 1, lanes] * SCALE
                held[lanes, :] = jnp.transpose(jnp.broadcast_to(line, (128, 128)))
            return carry

        lax.fori_loop(first, last, one, 0)

    place_cells(0, 8)

    for s in (1, 2, 3):
        ref = coords.at[1, p.z * XS + p.at_x(-s)]
        remote(ref, ref, c_send, c_recv.at[s], dev=p.dev).wait_recv()
    for s in range(1, ZS):
        ref = coords.at[1, pl.ds(p.z * XS, XS)]
        remote(ref, ref, cz_send, c_recv.at[3 + s], dev=z_peers[s - 1]).start()

    ga.round(1)
    gb.round(1)
    place_cells(8, 20)

    for s in range(1, ZS):
        ref = coords.at[1, pl.ds(p.at_z(-s) * XS, XS)]
        remote(ref, ref, cz_send, c_recv.at[3 + s], dev=p.dev).wait_recv()
    coord_ahead = remote(coords.at[1], coords.at[0], cc_send, c_recv.at[0], cont=p.ahead)
    coord_ahead.start()

    ga.round(2)
    gb.round(2)
    place_cells(20, CELLS // 128)
    rain_copy.wait()
    rain_win[...] = jnp.zeros_like(rain_win)
    rain_win[WOFF : WOFF + WIN, :] = rain_raw[...]
    coord_ahead.wait_recv()

    def listed(t, k):
        block = tiles[t, k]
        own = jnp.where(block // GROUP == p.cont, 1, 0)
        dev = block % GROUP
        return own, dev % ZS * XS + dev // ZS, dev

    def cover(first, last):
        def one(g, carry):
            t, k = g // LISTED, g % LISTED
            own, at, _ = listed(t, k)
            sx, sy = coords[own, at, 0:1, :], coords[own, at, 1:2, :]
            lanes = pl.ds(pl.multiple_of(k * BS, BS), BS)

            def part(c, carry):
                rows = pl.ds(pl.multiple_of(t * TILE + c * 256, 256), 256)
                dx = cellx[rows, :] - sx
                dy = celly[rows, :] - sy
                square = dx * dx + dy * dy + NUGGET
                cov[rows, lanes] = jnp.exp2(-4.0 - square * lax.rsqrt(square)).astype(BF16)
                return carry

            return lax.fori_loop(0, TILE // 256, part, carry)

        lax.fori_loop(first, last, one, 0)

    cover(0, 3)
    done = 3
    for r in (3, 4, 5, 6):
        ga.round(r)
        cover(done, done + 4)
        gb.round(r)
        cover(done + 4, done + 8)
        done += 8

    for k in range(NCOND):
        dev = cond[0, k] % GROUP
        prior[k * BS : k * BS + HALF, :] = sva[dev % ZS * XS + dev // ZS]
        prior[k * BS + HALF : (k + 1) * BS, :] = svb[dev]
    predicted = dot(weights[0], prior[...])
    values = jnp.concatenate([sva[slot_a], svb[slot_b]], axis=0).astype(F32)
    innovation = (values - predicted).astype(BF16)
    whitened = dot(factor[0], innovation).astype(BF16)
    kweights = dot(factor[0], whitened, ((0,), (0,))).astype(BF16)
    kwa[1, slot_a] = kweights[:HALF]
    kwb[1, slot_b] = kweights[HALF:]

    ka = GatherA(p, kwa.at[1], ka_send, ka_recv)
    kb = GatherB(p, kwb.at[1], kb_send, kb_recv)
    kp = GatherB(p, kwb.at[0], kp_send, kp_recv)

    def inject():
        return remote(
            kwb.at[1, slot_b], kwb.at[0, slot_b], inj_send, inj_recv, cont=p.ahead
        )

    def ahead_a(i):
        part = pl.ds(p.zs[i] * XS, XS)
        return remote(kwa.at[1, part], kwa.at[0, part], fa_send, fa_recv.at[i], cont=p.ahead)

    def ahead_b(j):
        part = pl.ds(p.xs[j] * ZS, ZS)
        return remote(kwb.at[1, part], kwb.at[0, part], fb_send, fb_recv.at[j], cont=p.ahead)

    odd = jnp.logical_not(p.even)

    @pl.when(odd)
    def _():
        inject().start()

    ka.start()
    kb.start()
    left = TILES * LISTED - done
    spans = [done + left * i // 10 for i in range(11)]

    @pl.when(p.even)
    def _():
        inject().wait_recv()
        kp.start()

    cover(spans[0], spans[1])
    for r in range(1, 8):
        if r <= 6:
            ka.round(r)
            if r >= 2:
                for i in ((0,), (1, 2), (3, 4), (5, 6), (7,))[r - 2]:
                    ahead_a(i).start()
            if r <= 4:
                cover(spans[2 * r - 1], spans[2 * r])
            kb.round(r)

        @pl.when(p.even)
        def _(r=r):
            if r >= 2:
                kp.round(r - 1)
            for j in {4: (0,), 5: (1, 2), 6: (3,)}.get(r, ()):
                ahead_b(j).start()

        if r <= 4:
            cover(spans[2 * r], spans[2 * r + 1])
    cover(spans[9], spans[10])

    for i in range(ZS):
        ahead_a(i).wait_recv()

    @pl.when(odd)
    def _():
        for j in range(XS):
            ahead_b(j).wait_recv()

    for t in range(TILES):

        def choose(k, carry):
            own, at, dev = listed(t, k)
            chosen[pl.ds(pl.multiple_of(k * BS, BS), HALF), :] = kwa[own, at]
            chosen[pl.ds(pl.multiple_of(k * BS + HALF, HALF), HALF), :] = kwb[own, dev]
            return carry

        lax.fori_loop(0, LISTED, choose, 0)

        def part(c, carry):
            rows = pl.ds(pl.multiple_of(t * TILE + c * CHUNK, CHUNK), CHUNK)
            full = dot(cov[rows, :], chosen[...])
            out[rows, :] = full[:, :DAYS].astype(BF16)
            window = jnp.transpose(full[:, WLANE : WLANE + 128])[WROW : WROW + WROWS, :]
            soft = jnp.tanh((rain_win[:, rows] - window) * 2.0)
            row = lax.broadcasted_iota(jnp.int32, soft.shape, 0)
            soft = jnp.where((row >= WOFF) & (row < WOFF + WIN), soft, 0.0)
            total = jnp.sum(soft, axis=0, keepdims=True)
            share[:, rows] = total * (0.5 / WIN) + 0.5
            return carry

        lax.fori_loop(0, TILE // CHUNK, part, 0)

    ga.sent()
    gb.sent()
    ka.sent()
    kb.sent()
    ref = coords.at[1, pl.ds(0, 3)]
    remote(ref, ref, c_send, c_recv.at[0], dev=p.dev).wait_send()
    ref = coords.at[1, pl.ds(0, XS * (ZS - 1))]
    remote(ref, ref, cz_send, c_recv.at[0], dev=p.dev).wait_send()
    coord_ahead.wait_send()
    ref = kwa.at[1]
    remote(ref, ref, fa_send, fa_recv.at[0], dev=p.dev).wait_send()

    @pl.when(odd)
    def _():
        inject().wait_send()

    @pl.when(p.even)
    def _():
        kp.sent()
        ref = kwb.at[1]
        remote(ref, ref, fb_send, fb_recv.at[0], dev=p.dev).wait_send()


def per_device(sv, weights, factor, cond, xy, cells, tiles, rain):
    dma = pltpu.SemaphoreType.DMA
    vmem, smem = pl.BlockSpec(memory_space=pltpu.VMEM), pl.BlockSpec(memory_space=pltpu.SMEM)
    thresholds, share = pl.pallas_call(
        kernel,
        out_shape=(
            jax.ShapeDtypeStruct((CELLS, DAYS), BF16),
            jax.ShapeDtypeStruct((1, CELLS), F32),
        ),
        in_specs=[smem, smem, vmem, vmem, vmem, vmem, vmem, pl.BlockSpec(memory_space=pl.ANY)],
        out_specs=(vmem, vmem),
        scratch_shapes=[
            pltpu.VMEM((GROUP, HALF, COLS), BF16),
            pltpu.VMEM((GROUP, HALF, COLS), BF16),
            pltpu.VMEM((2, GROUP, HALF, COLS), BF16),
            pltpu.VMEM((2, GROUP, HALF, COLS), BF16),
            pltpu.VMEM((2, GROUP, 8, BS), F32),
            pltpu.VMEM((CELLS, 128), F32),
            pltpu.VMEM((CELLS, 128), F32),
            pltpu.VMEM((WIN, CELLS), F32),
            pltpu.VMEM((WROWS, CELLS), F32),
            pltpu.VMEM((NCOND * BS, COLS), BF16),
            pltpu.VMEM((CELLS, STATIONS), BF16),
            pltpu.VMEM((STATIONS, COLS), BF16),
            dma,
            dma, dma((3 + ZS,)), dma, dma,
            dma, dma((A_SEMS,)), dma, dma((B_SEMS,)),
            dma, dma((A_SEMS,)), dma, dma((B_SEMS,)), dma, dma((B_SEMS,)),
            dma, dma((ZS,)), dma, dma((XS,)), dma, dma,
        ],
        compiler_params=pltpu.CompilerParams(
            collective_id=0, has_side_effects=True, vmem_limit_bytes=56 * 1024 * 1024
        ),
    )(cond, tiles, sv, weights, factor, xy, cells, rain)
    return thresholds, share.reshape(-1)


def solution(mesh):
    both = ("cont", "dev")
    placed = (
        P(both, None, None),
        P(both, None, None),
        P(both, None, None),
        P(both, None),
        P(both, None, None),
        P(None, both),
        P(both, None),
        P(None, both),
    )
    return jax.shard_map(
        per_device,
        mesh=mesh,
        in_specs=placed,
        out_specs=(P(both, None), P(both)),
        check_vma=False,
    )
```

```python
import heapq
import math

import jax
import jax.numpy as jnp
from jax import lax
from jax.experimental import pallas as pl
from jax.experimental.pallas import tpu as pltpu
from jax.sharding import PartitionSpec as P

MESH = pl.DeviceIdType.MESH
BF16 = jnp.bfloat16
F32 = jnp.float32

XS, ZS = 4, 8
GROUP = XS * ZS
CONTS = 8
BS = 128
DAYS = 366
ROWS = 368
ROWS_A, CUT_A = 160, 80
ROWS_B, CUT_B = ROWS - ROWS_A, 112
NCOND = 4
LISTED = 16
STATIONS = LISTED * BS
TILES = 4
TILE = 1024
CELLS = TILES * TILE
WIN = 60
WSTART = 150
WROW = WSTART // 8 * 8
WOFF = WSTART - WROW
WROWS = -(-(WOFF + WIN) // 8) * 8
LENGTH = 9.0 * STATIONS**-0.5
SCALE = math.log2(math.e) / LENGTH
NUGGET = (LENGTH * 0.1 * SCALE) ** 2
CHUNK = 512


class Place:
    def __init__(self):
        self.dev, self.cont = lax.axis_index("dev"), lax.axis_index("cont")
        self.x, self.z = self.dev // ZS, self.dev % ZS
        self.xs = {s: lax.rem(self.x + (s + XS), XS) for s in (-1, 0, 1, 2)}
        self.zs = {s: lax.rem(self.z + (s + ZS), ZS) for s in (-3, -2, -1, 0, 1, 2, 3, 4)}
        self.ahead = lax.rem(self.cont + 1, CONTS)
        self.behind = lax.rem(self.cont + CONTS - 1, CONTS)
        self.even = lax.rem(self.cont, 2) == 0

    def toward(self, way):
        axis, step = way
        if axis == "cont":
            return {"cont": self.ahead}
        x, z = (self.xs[step], self.z) if axis == "x" else (self.x, self.zs[step])
        return {"dev": x * ZS + z}


def remote(src, dst, send, recv, device):
    return pltpu.make_async_remote_copy(
        src_ref=src, dst_ref=dst, send_sem=send, recv_sem=recv, device_id=device, device_id_type=MESH
    )


def along_x_first(item):
    dx, dz, part = item
    sends = []
    if dz == 0:
        if dx == 0:
            sends += [(("x", s), (-s, 0, 0)) for s in (1, -1)] + [(("x", 2), (2, 0, 0))]
        sends += [(("z", s), (dx, -s, 0)) for s in (1, -1)]
    elif abs(dz) < 3 or (abs(dz) == 3 and (dz < 0) == (dx in (0, 1))):
        step = 1 if dz < 0 else -1
        far = dz - step
        sends.append((("z", step), (dx, 4 if abs(far) == 4 else far, 0)))
    return sends


def along_z_first(item):
    dx, dz, part = item
    sends = []
    if dx == 0:
        if dz == 0:
            sends += [(("z", s), (0, -s, 0)) for s in (1, -1)]
        elif abs(dz) < 3:
            step = 1 if dz < 0 else -1
            sends.append((("z", step), (0, dz - step, 0)))
        elif abs(dz) == 3:
            step = 1 if dz < 0 else -1
            sends.append((("z", step), (0, 4, step)))
        sends += [(("x", s), (-s, dz, 0)) for s in (1, -1)]
        if dz == 4:
            sends.append((("x", 2), (2, 4, 0)))
    elif dx != 2 and dz != 4:
        if dz == 0:
            sends.append((("x", -dx), (2, 0, dx)))
        elif (dz < 0) == (dx < 0):
            sends.append((("x", -dx), (2, dz, 0)))
    return sends


def items_of(sends_of):
    found, todo = [], [(0, 0, 0)]
    while todo:
        item = todo.pop(0)
        found.append(item)
        if item[2] == 0:
            todo += [arrival for _, arrival in sends_of(item)]
        elif (*item[:2], 0) not in found:
            todo.append((*item[:2], 0))
            found.append((*item[:2], 0))
            todo.pop()
            todo += [arrival for _, arrival in sends_of((*item[:2], 0))]
    return list(dict.fromkeys(found))


SENDS = {"a": along_x_first, "b": along_z_first}
ITEMS = {kind: items_of(sends) for kind, sends in SENDS.items()}
SEM = {kind: {item: i for i, item in enumerate(items)} for kind, items in ITEMS.items()}
HALF_ROWS = {"a": ROWS_A, "b": ROWS_B}
CUT = {"a": CUT_A, "b": CUT_B}


class Gather:
    def __init__(self, place, kind, buf, send, recv):
        self.place, self.kind, self.buf, self.send, self.recv = place, kind, buf, send, recv

    def ref(self, item):
        dx, dz, part = item
        x, z = self.place.xs[dx], self.place.zs[dz]
        slot = z * XS + x if self.kind == "a" else x * ZS + z
        if part == 0:
            return self.buf.at[slot]
        first, last = (0, CUT[self.kind]) if part < 0 else (CUT[self.kind], HALF_ROWS[self.kind])
        return self.buf.at[slot, pl.ds(first, last - first)]

    def pass_on(self, item):
        for way, arrival in SENDS[self.kind](item):
            ref = self.ref((*item[:2], arrival[2]))
            sem = self.recv.at[SEM[self.kind][arrival]]
            remote(ref, ref, self.send, sem, self.place.toward(way)).start()

    def arrive(self, item):
        ref = self.ref(item)
        sem = self.recv.at[SEM[self.kind][item]]
        remote(ref, ref, self.send, sem, {"dev": self.place.dev}).wait_recv()

    def sent(self):
        ref = self.buf.at[pl.ds(0, GROUP - 1)]
        remote(ref, ref, self.send, self.recv.at[0], {"dev": self.place.dev}).wait_send()


RATE, HOP, MORE, CORE_RATE, CORE_HOP, ISSUE = 92e3, 2.64, 0.62, 1.4e6, 0.75, 0.04
KRIGING = 0.8
STEP_COST = 0.28
READY = 14.0


def schedule():
    links, queue, clock = {}, [], [0.0, 0.0]
    plan, whole, got, count = [], {}, {}, 0
    left = [TILES * LISTED] * 2

    def post(core, way, size, target, arrival):
        nonlocal count
        clock[core] += ISSUE
        end = clock[core]
        if way == ("cont", 0):
            end += size / CORE_RATE + CORE_HOP
        else:
            lanes = [(way[0], 1), (way[0], -1)] if way[1] == 2 else [way]
            for lane in lanes:
                links[lane] = max(clock[core], links.get(lane, 0.0)) + size / RATE
                end = max(end, links[lane])
            end += HOP + (MORE if way[1] == 2 else 0.0)
        count += 1
        heapq.heappush(queue, (end, count, target, arrival))

    def forward(core, stage, kind, source, item):
        size = HALF_ROWS[kind] * BS * 2
        if kind == "b" and core == 1 and stage == "kw" and item == (0, 0, 0):
            post(1, ("y", 1), size, 0, (stage, kind, "prev", item))
        if source == "own" or (kind == "b" and core == 0):
            for way, arrival in SENDS[kind](item):
                part = size if arrival[2] == 0 else size / 2
                post(core, way, part, core, (stage, kind, source, arrival))
        if source == "own" and stage == "kw" and (kind == "a" or core == 0):
            way = ("cont", 0) if core == 0 else ("y", 1)
            post(core, way, size, 1 - core, (stage, kind, "prev", item))

    for kind in ("b", "a"):
        for core in (0, 1):
            forward(core, "sv", kind, "own", (0, 0, 0))
    while queue:
        when, _, core, (stage, kind, source, item) = heapq.heappop(queue)
        passive = source == "prev" and (kind == "a" or core == 1)
        if passive:
            continue
        while left[core] and when - max(clock[core], READY) > STEP_COST / 4:
            clock[core] = max(clock[core], READY) + STEP_COST
            left[core] -= 1
            if core == 0 and plan[-1][0] == "cover":
                plan[-1] = ("cover", plan[-1][1] + 1)
            elif core == 0:
                plan.append(("cover", 1))
        clock[core] = max(clock[core], when) + ISSUE
        if core == 0:
            plan.append(("arrive", stage, kind, source, item, clock[0]))
        if item[2]:
            item = (*item[:2], 0)
            key = (core, stage, kind, source, item)
            whole[key] = whole.get(key, 0) + 1
            if whole[key] < 2:
                continue
        if core == 0:
            plan.append(("pass", stage, kind, source, item, clock[0]))
        forward(core, stage, kind, source, item)
        if stage == "sv":
            got[core, kind] = got.get((core, kind), 1) + 1
            if got[core, kind] == GROUP:
                clock[core] += KRIGING
                if core == 0:
                    plan.append(("krige", kind))
                forward(core, "kw", kind, "own", (0, 0, 0))
    plan.append(("cover", left[0]))
    return plan


def dot(a, b, dims=((1,), (0,))):
    return lax.dot_general(a, b, (dims, ((), ())), preferred_element_type=F32)


def kernel(
    cond, tiles, sv, weights, factor, xy, cells, rain,
    out, share,
    sva, svb, kwa, kwb, coords, cellx, celly, rain_raw, rain_win, prior, cov, chosen,
    rain_sem,
    c_send, c_recv, cz_send, cc_send,
    sa_send, sa_recv, sb_send, sb_recv,
    ka_send, ka_recv, kb_send, kb_recv, kp_send, kp_recv,
    fa_send, fa_recv, fb_send, fb_recv, inj_send, inj_recv,
):
    p = Place()
    odd = jnp.logical_not(p.even)
    slot_a, slot_b = p.z * XS + p.x, p.dev
    here = {"dev": p.dev}
    gathers = {
        ("sv", "a", "own"): Gather(p, "a", sva, sa_send, sa_recv),
        ("sv", "b", "own"): Gather(p, "b", svb, sb_send, sb_recv),
        ("kw", "a", "own"): Gather(p, "a", kwa.at[1], ka_send, ka_recv),
        ("kw", "b", "own"): Gather(p, "b", kwb.at[1], kb_send, kb_recv),
        ("kw", "b", "prev"): Gather(p, "b", kwb.at[0], kp_send, kp_recv),
    }
    rain_copy = pltpu.make_async_copy(rain, rain_raw, rain_sem)
    rain_copy.start()

    barrier = pltpu.get_barrier_semaphore()
    x_ways = [("x", s) for s in (1, -1, 2)]
    z_ways = [("z", s) for s in (1, -1, 2, -2, 3, -3, 4)]
    for way in x_ways + z_ways:
        pl.semaphore_signal(barrier, inc=1, device_id=p.toward(way), device_id_type=MESH)
    pl.semaphore_signal(barrier, inc=1, device_id={"cont": p.behind}, device_id_type=MESH)

    sva[slot_a] = sv[0, :ROWS_A, :]
    svb[slot_b] = jnp.concatenate(
        [sv[0, ROWS_A:, :], jnp.zeros((ROWS - DAYS, BS), BF16)], axis=0
    )
    coords[1, slot_a] = jnp.concatenate(
        [xy[0].astype(F32) * SCALE, jnp.zeros((6, BS), F32)], axis=0
    )
    pl.semaphore_wait(barrier, XS + ZS - 1)

    own = coords.at[1, slot_a]
    for i, way in enumerate(x_ways):
        remote(own, own, c_send, c_recv.at[i], p.toward(way)).start()
    for kind in ("b", "a"):
        gathers["sv", kind, "own"].pass_on((0, 0, 0))

    def coords_x():
        for i, (_, s) in enumerate(x_ways):
            ref = coords.at[1, p.z * XS + p.xs[2 if s == 2 else -s]]
            remote(ref, ref, c_send, c_recv.at[i], here).wait_recv()
        ref = coords.at[1, pl.ds(p.z * XS, XS)]
        for i, way in enumerate(z_ways):
            remote(ref, ref, cz_send, c_recv.at[3 + i], p.toward(way)).start()

    coord_ahead = remote(coords.at[1], coords.at[0], cc_send, c_recv.at[10], {"cont": p.ahead})

    def coords_z():
        for i, (_, s) in enumerate(z_ways):
            ref = coords.at[1, pl.ds(p.zs[4 if s == 4 else -s] * XS, XS)]
            remote(ref, ref, cz_send, c_recv.at[3 + i], here).wait_recv()
        coord_ahead.start()

    def place_cells(first, last):
        def one(c, carry):
            lanes = pl.ds(pl.multiple_of(c * 128, 128), 128)
            for row, held in ((0, cellx), (1, celly)):
                line = cells[row : row + 1, lanes] * SCALE
                held[lanes, :] = jnp.transpose(jnp.broadcast_to(line, (128, 128)))
            return carry

        lax.fori_loop(first, last, one, 0)

    def place_rain():
        rain_copy.wait()
        rain_win[...] = jnp.zeros_like(rain_win)
        rain_win[WOFF : WOFF + WIN, :] = rain_raw[...]

    def listed(t, k):
        block = tiles[t, k]
        own = jnp.where(block // GROUP == p.cont, 1, 0)
        dev = block % GROUP
        return own, dev % ZS * XS + dev // ZS, dev

    def cover(first, last):
        def one(g, carry):
            t, k = g // LISTED, g % LISTED
            own, at, _ = listed(t, k)
            sx, sy = coords[own, at, 0:1, :], coords[own, at, 1:2, :]
            lanes = pl.ds(pl.multiple_of(k * BS, BS), BS)

            def part(c, carry):
                rows = pl.ds(pl.multiple_of(t * TILE + c * 256, 256), 256)
                dx = cellx[rows, :] - sx
                dy = celly[rows, :] - sy
                square = dx * dx + dy * dy + NUGGET
                cov[rows, lanes] = jnp.exp2(-4.0 - square * lax.rsqrt(square)).astype(BF16)
                return carry

            return lax.fori_loop(0, TILE // 256, part, carry)

        lax.fori_loop(first, last, one, 0)

    def krige(kind):
        buf, slot = (sva, slot_a) if kind == "a" else (svb, slot_b)
        rows = pl.ds(0, HALF_ROWS[kind])
        for k in range(NCOND):
            dev = cond[0, k] % GROUP
            at = dev % ZS * XS + dev // ZS if kind == "a" else dev
            prior[rows, k * BS : (k + 1) * BS] = buf[at]
        predicted = dot(prior[rows, :], weights[0], ((1,), (1,)))
        innovation = (buf[slot].astype(F32) - predicted).astype(BF16)
        whitened = dot(innovation, factor[0], ((1,), (1,))).astype(BF16)
        kweights = dot(whitened, factor[0]).astype(BF16)
        if kind == "a":
            kwa[1, slot_a] = kweights
        else:
            kwb[1, slot_b] = kweights

            @pl.when(odd)
            def _():
                remote(
                    kwb.at[1, slot_b], kwb.at[0, slot_b], inj_send, inj_recv, {"cont": p.ahead}
                ).start()

    def lend(kind, item):
        buf, send, recv = (kwa, fa_send, fa_recv) if kind == "a" else (kwb, fb_send, fb_recv)
        x, z = p.xs[item[0]], p.zs[item[1]]
        slot = z * XS + x if kind == "a" else x * ZS + z
        remote(buf.at[1, slot], buf.at[0, slot], send, recv, {"cont": p.ahead}).start()

    def pass_on(stage, kind, source, item):
        gathers[stage, kind, source].pass_on(item)
        if stage == "kw" and source == "own":
            if kind == "a":
                lend(kind, item)
            else:
                pl.when(p.even)(lambda: lend(kind, item))

    def act(step):
        what, stage, kind, source, item, _ = step
        if what == "arrive":
            if source == "prev" and item == (0, 0, 0):
                ref = kwb.at[0, slot_b]
                remote(ref, ref, inj_send, inj_recv, here).wait_recv()
            else:
                gathers[stage, kind, source].arrive(item)
        else:
            pass_on(stage, kind, source, item)

    early = [
        (1.0, lambda: place_cells(0, 8)),
        (3.4, coords_x),
        (4.0, lambda: place_cells(8, 16)),
        (7.0, lambda: place_cells(16, 24)),
        (9.0, coords_z),
        (9.0, lambda: place_cells(24, CELLS // 128)),
        (READY - 1.0, place_rain),
        (READY - 1.0, coord_ahead.wait_recv),
    ]
    done = 0
    steps = schedule()
    while steps:
        step = steps.pop(0)
        if step[0] == "cover":
            cover(done, done + step[1])
            done += step[1]
        elif step[0] == "krige":
            krige(step[1])
            pass_on("kw", step[1], "own", (0, 0, 0))
        else:
            while early and early[0][0] < step[5]:
                early.pop(0)[1]()
            batch = [step]
            if step[3] == "prev":
                while steps and steps[0][0] in ("arrive", "pass") and steps[0][3] == "prev":
                    batch.append(steps.pop(0))

                @pl.when(p.even)
                def _(batch=batch):
                    for one in batch:
                        act(one)
            else:
                act(step)

    whole = kwa.at[0]
    remote(whole, whole, fa_send, fa_recv, here).wait_recv()

    @pl.when(odd)
    def _():
        ref = kwb.at[0]
        remote(ref, ref, fb_send, fb_recv, here).wait_recv()

    for t in range(TILES):

        def choose(k, carry):
            own, at, dev = listed(t, k)
            lanes = pl.ds(pl.multiple_of(k * BS, BS), BS)
            chosen[:ROWS_A, lanes] = kwa[own, at]
            chosen[ROWS_A:, lanes] = kwb[own, dev]
            return carry

        lax.fori_loop(0, LISTED, choose, 0)

        def part(c, carry):
            at = pl.ds(pl.multiple_of(t * TILE + c * CHUNK, CHUNK), CHUNK)
            full = dot(chosen[...], cov[at, :], ((1,), (1,)))
            out[:, at] = full[:DAYS].astype(BF16)
            soft = jnp.tanh((rain_win[:, at] - full[WROW : WROW + WROWS]) * 2.0)
            row = lax.broadcasted_iota(jnp.int32, soft.shape, 0)
            soft = jnp.where((row >= WOFF) & (row < WOFF + WIN), soft, 0.0)
            total = jnp.sum(soft, axis=0, keepdims=True)
            share[:, at] = total * (0.5 / WIN) + 0.5
            return carry

        lax.fori_loop(0, TILE // CHUNK, part, 0)

    for (_, _, source), gather in gathers.items():
        if source == "own":
            gather.sent()
    ref = coords.at[1, pl.ds(0, XS - 1)]
    remote(ref, ref, c_send, c_recv.at[0], here).wait_send()
    ref = coords.at[1, pl.ds(0, XS * (ZS - 1))]
    remote(ref, ref, cz_send, c_recv.at[0], here).wait_send()
    coord_ahead.wait_send()
    remote(whole, whole, fa_send, fa_recv, here).wait_send()

    @pl.when(odd)
    def _():
        remote(
            kwb.at[1, slot_b], kwb.at[0, slot_b], inj_send, inj_recv, {"cont": p.ahead}
        ).wait_send()

    @pl.when(p.even)
    def _():
        gathers["kw", "b", "prev"].sent()
        ref = kwb.at[1]
        remote(ref, ref, fb_send, fb_recv, here).wait_send()


def per_device(sv, weights, factor, cond, xy, cells, tiles, rain):
    dma = pltpu.SemaphoreType.DMA
    vmem, smem = pl.BlockSpec(memory_space=pltpu.VMEM), pl.BlockSpec(memory_space=pltpu.SMEM)
    thresholds, share = pl.pallas_call(
        kernel,
        out_shape=(
            jax.ShapeDtypeStruct((DAYS, CELLS), BF16),
            jax.ShapeDtypeStruct((1, CELLS), F32),
        ),
        in_specs=[smem, smem, vmem, vmem, vmem, vmem, vmem, pl.BlockSpec(memory_space=pl.ANY)],
        out_specs=(vmem, vmem),
        scratch_shapes=[
            pltpu.VMEM((GROUP, ROWS_A, BS), BF16),
            pltpu.VMEM((GROUP, ROWS_B, BS), BF16),
            pltpu.VMEM((2, GROUP, ROWS_A, BS), BF16),
            pltpu.VMEM((2, GROUP, ROWS_B, BS), BF16),
            pltpu.VMEM((2, GROUP, 8, BS), F32),
            pltpu.VMEM((CELLS, 128), F32),
            pltpu.VMEM((CELLS, 128), F32),
            pltpu.VMEM((WIN, CELLS), F32),
            pltpu.VMEM((WROWS, CELLS), F32),
            pltpu.VMEM((ROWS, NCOND * BS), BF16),
            pltpu.VMEM((CELLS, STATIONS), BF16),
            pltpu.VMEM((ROWS, STATIONS), BF16),
            dma,
            dma, dma((XS + ZS - 1,)), dma, dma,
            dma, dma((len(ITEMS["a"]),)), dma, dma((len(ITEMS["b"]),)),
            dma, dma((len(ITEMS["a"]),)), dma, dma((len(ITEMS["b"]),)), dma, dma((len(ITEMS["b"]),)),
            dma, dma, dma, dma, dma, dma,
        ],
        compiler_params=pltpu.CompilerParams(
            collective_id=0, has_side_effects=True, vmem_limit_bytes=56 * 1024 * 1024
        ),
    )(cond, tiles, jnp.swapaxes(sv, 1, 2), weights, factor, xy, cells, rain)
    return thresholds.T, share.reshape(-1)


def solution(mesh):
    both = ("cont", "dev")
    placed = (
        P(both, None, None),
        P(both, None, None),
        P(both, None, None),
        P(both, None),
        P(both, None, None),
        P(None, both),
        P(both, None),
        P(None, both),
    )
    return jax.shard_map(
        per_device,
        mesh=mesh,
        in_specs=placed,
        out_specs=(P(both, None), P(both)),
        check_vma=False,
    )
```

```python
import heapq
import math

import jax
import jax.numpy as jnp
from jax import lax
from jax.experimental import pallas as pl
from jax.experimental.pallas import tpu as pltpu
from jax.sharding import PartitionSpec as P

MESH = pl.DeviceIdType.MESH
BF16 = jnp.bfloat16
F32 = jnp.float32

XS, ZS = 4, 8
GROUP = XS * ZS
CONTS = 8
BS = 128
DAYS = 366
ROWS = 368
SV_A, KW_A = 176, 192
NCOND = 4
LISTED = 16
STATIONS = LISTED * BS
TILES = 4
TILE = 1024
CELLS = TILES * TILE
WIN = 60
WSTART = 150
WROW = WSTART // 8 * 8
WOFF = WSTART - WROW
WROWS = -(-(WOFF + WIN) // 8) * 8
LENGTH = 9.0 * STATIONS**-0.5
SCALE = math.log2(math.e) / LENGTH
NUGGET = (LENGTH * 0.1 * SCALE) ** 2


class Place:
    def __init__(self):
        self.dev, self.cont = lax.axis_index("dev"), lax.axis_index("cont")
        self.x, self.z = self.dev // ZS, self.dev % ZS
        self.xs = {s: lax.rem(self.x + (s + XS), XS) for s in (-1, 0, 1, 2)}
        self.zs = {s: lax.rem(self.z + (s + ZS), ZS) for s in (-3, -2, -1, 0, 1, 2, 3, 4)}
        self.ahead = lax.rem(self.cont + 1, CONTS)
        self.behind = lax.rem(self.cont + CONTS - 1, CONTS)
        self.even = lax.rem(self.cont, 2) == 0

    def toward(self, way):
        axis, step = way
        if axis == "cont":
            return {"cont": self.ahead}
        x, z = (self.xs[step], self.z) if axis == "x" else (self.x, self.zs[step])
        return {"dev": x * ZS + z}


def remote(src, dst, send, recv, device):
    return pltpu.make_async_remote_copy(
        src_ref=src, dst_ref=dst, send_sem=send, recv_sem=recv, device_id=device, device_id_type=MESH
    )


def along_x_first(item):
    dx, dz, part = item
    sends = []
    if dz == 0:
        if dx == 0:
            sends += [(("x", s), (-s, 0, 0)) for s in (1, -1)] + [(("x", 2), (2, 0, 0))]
        sends += [(("z", s), (dx, -s, 0)) for s in (1, -1)]
    elif abs(dz) < 3 or (abs(dz) == 3 and (dz < 0) == (dx in (0, 1))):
        step = 1 if dz < 0 else -1
        far = dz - step
        sends.append((("z", step), (dx, 4 if abs(far) == 4 else far, 0)))
    return sends


def along_z_first(item):
    dx, dz, part = item
    sends = []
    if dx == 0:
        if dz == 0:
            sends += [(("z", s), (0, -s, 0)) for s in (1, -1)]
        elif abs(dz) < 3:
            step = 1 if dz < 0 else -1
            sends.append((("z", step), (0, dz - step, 0)))
        elif abs(dz) == 3:
            step = 1 if dz < 0 else -1
            sends.append((("z", step), (0, 4, step)))
        sends += [(("x", s), (-s, dz, 0)) for s in (1, -1)]
        if dz == 4:
            sends.append((("x", 2), (2, 4, 0)))
    elif dx != 2 and dz != 4:
        if dz == 0:
            sends.append((("x", -dx), (2, 0, dx)))
        elif (dz < 0) == (dx < 0):
            sends.append((("x", -dx), (2, dz, 0)))
    return sends


def items_of(sends_of):
    found, todo = [], [(0, 0, 0)]
    while todo:
        item = todo.pop(0)
        found.append(item)
        if item[2] == 0:
            todo += [arrival for _, arrival in sends_of(item)]
        elif (*item[:2], 0) not in found:
            todo.append((*item[:2], 0))
            found.append((*item[:2], 0))
            todo.pop()
            todo += [arrival for _, arrival in sends_of((*item[:2], 0))]
    return list(dict.fromkeys(found))


SENDS = {"a": along_x_first, "b": along_z_first}
ITEMS = {kind: items_of(sends) for kind, sends in SENDS.items()}
SEM = {kind: {item: i for i, item in enumerate(items)} for kind, items in ITEMS.items()}
HALF_ROWS = {"sv": {"a": SV_A, "b": ROWS - SV_A}, "kw": {"a": KW_A, "b": ROWS - KW_A}}


class Gather:
    def __init__(self, place, kind, buf, send, recv):
        self.place, self.kind, self.buf, self.send, self.recv = place, kind, buf, send, recv
        self.rows = buf.shape[1]

    def ref(self, item):
        dx, dz, part = item
        x, z = self.place.xs[dx], self.place.zs[dz]
        slot = z * XS + x if self.kind == "a" else x * ZS + z
        if part == 0:
            return self.buf.at[slot]
        cut = self.rows // 32 * 16
        first, last = (0, cut) if part < 0 else (cut, self.rows)
        return self.buf.at[slot, pl.ds(first, last - first)]

    def send_on(self, item, index):
        way, arrival = SENDS[self.kind](item)[index]
        ref = self.ref((*item[:2], arrival[2]))
        sem = self.recv.at[SEM[self.kind][arrival]]
        remote(ref, ref, self.send, sem, self.place.toward(way)).start()

    def arrive(self, item):
        ref = self.ref(item)
        sem = self.recv.at[SEM[self.kind][item]]
        remote(ref, ref, self.send, sem, {"dev": self.place.dev}).wait_recv()

    def sent(self):
        ref = self.buf.at[pl.ds(0, GROUP - 1)]
        remote(ref, ref, self.send, self.recv.at[0], {"dev": self.place.dev}).wait_send()


RATE, HOP, MORE, CORE_RATE, CORE_HOP, ISSUE = 92e3, 3.2, 0.62, 1.4e6, 0.75, 0.08
KRIGING = 0.8
STEP_COST = 0.28
READY = 14.0


LEND = {"a": XS, "b": ZS}
DEPTH = 1.0


def chain(kind, item):
    return max([1 + chain(kind, (*to[:2], 0)) for _, to in SENDS[kind](item)], default=0)


def schedule():
    links, queue, clock = {}, [], [0.0, 0.0]
    plan, whole, got, lent, count = [], {}, {}, {}, 0
    left = [TILES * LISTED] * 2
    waiting = ([], [])

    def post(core, way, size, target, arrival):
        nonlocal count
        clock[core] += ISSUE
        end = clock[core]
        if way == ("cont", 0):
            end += size / CORE_RATE + CORE_HOP
        else:
            lanes = [(way[0], 1), (way[0], -1)] if way[1] == 2 else [way]
            for lane in lanes:
                links[lane] = max(clock[core], links.get(lane, 0.0)) + size / RATE
                end = max(end, links[lane])
            end += HOP + (MORE if way[1] == 2 else 0.0)
        count += 1
        heapq.heappush(queue, (end, count, target, arrival))

    def flush(core):
        later = []
        soon = queue[0][0] if queue else 1e9
        for entry in sorted(waiting[core]):
            _, _, index, stage, kind, source, item = entry
            way, arrival = SENDS[kind](item)[index]
            lanes = [(way[0], 1), (way[0], -1)] if way[1] == 2 else [way]
            free = min(links.get(lane, 0.0) for lane in lanes)
            if free > max(clock[core] + DEPTH, soon):
                later.append(entry)
                continue
            size = HALF_ROWS[stage][kind] * BS * 2
            post(core, way, size if arrival[2] == 0 else size / 2, core, (stage, kind, source, arrival))
            if core == 0:
                plan.append(("send", stage, kind, source, item, clock[0], index))
        waiting[core][:] = later

    def forward(core, stage, kind, source, item):
        nonlocal count
        size = HALF_ROWS[stage][kind] * BS * 2
        if kind == "b" and core == 1 and stage == "kw" and item == (0, 0, 0):
            post(1, ("y", 1), size, 0, (stage, kind, "prev", item))
        if source == "own" or (kind == "b" and core == 0):
            for index, (way, arrival) in enumerate(SENDS[kind](item)):
                count += 1
                ahead = chain(kind, (*arrival[:2], 0))
                waiting[core].append((-ahead, count, index, stage, kind, source, item))
        if source == "own" and stage == "kw" and (kind == "a" or core == 0):
            group = item[1] if kind == "a" else item[0]
            size *= LEND[kind]
            have = lent[core, kind, group] = lent.get((core, kind, group), 0) + 1
            if have % LEND[kind]:
                return
            way = ("cont", 0) if core == 0 else ("y", 1)
            post(core, way, size, 1 - core, (stage, kind, "prev", item))
            if core == 0:
                plan.append(("lend", stage, kind, source, item, clock[0]))

    for kind in ("b", "a"):
        for core in (0, 1):
            forward(core, "sv", kind, "own", (0, 0, 0))
    while queue or waiting[0] or waiting[1]:
        for core in (0, 1):
            flush(core)
        if not queue:
            continue
        when, _, core, (stage, kind, source, item) = heapq.heappop(queue)
        passive = source == "prev" and (kind == "a" or core == 1)
        if passive:
            continue
        while left[core] and when - max(clock[core], READY) > STEP_COST / 4:
            clock[core] = max(clock[core], READY) + STEP_COST
            left[core] -= 1
            if core == 0 and plan[-1][0] == "cover":
                plan[-1] = ("cover", plan[-1][1] + 1)
            elif core == 0:
                plan.append(("cover", 1))
            flush(core)
        clock[core] = max(clock[core], when) + ISSUE
        if core == 0:
            plan.append(("arrive", stage, kind, source, item, clock[0]))
        if item[2]:
            item = (*item[:2], 0)
            key = (core, stage, kind, source, item)
            whole[key] = whole.get(key, 0) + 1
            if whole[key] < 2:
                continue
        forward(core, stage, kind, source, item)
        if stage == "sv":
            got[core, kind] = got.get((core, kind), 1) + 1
            ready = []
            if kind == "b" and got[core, "b"] == GROUP:
                ready.append("b")
            if got.get((core, "a")) == got.get((core, "b")) == GROUP:
                ready.append("a")
            for half in ready:
                clock[core] += KRIGING
                if core == 0:
                    plan.append(("krige", half))
                forward(core, "kw", half, "own", (0, 0, 0))
    plan.append(("cover", left[0]))
    return plan


def dot(a, b, dims=((1,), (0,))):
    return lax.dot_general(a, b, (dims, ((), ())), preferred_element_type=F32)


def kernel(
    cond_hbm, tiles_hbm, sv_hbm, weights_hbm, factor_hbm, xy_hbm, cells_hbm, rain,
    out, share,
    cond, tiles, sv, weights, factor, xy, cells, in_sem,
    sva, svb, kwa, kwb, row_coords, coords, cellx, celly, rain_raw, rain_win, prior, cov, chosen_a, chosen_b,
    rain_sem,
    c_send, c_recv, cz_send, cc_send,
    sa_send, sa_recv, sb_send, sb_recv,
    ka_send, ka_recv, kb_send, kb_recv, kp_send, kp_recv,
    fa_send, fa_recv, fb_send, fb_recv, inj_send, inj_recv,
):
    p = Place()
    odd = jnp.logical_not(p.even)
    slot_a, slot_b = p.z * XS + p.x, p.dev
    here = {"dev": p.dev}
    gathers = {
        ("sv", "a", "own"): Gather(p, "a", sva, sa_send, sa_recv),
        ("sv", "b", "own"): Gather(p, "b", svb, sb_send, sb_recv),
        ("kw", "a", "own"): Gather(p, "a", kwa.at[1], ka_send, ka_recv),
        ("kw", "b", "own"): Gather(p, "b", kwb.at[1], kb_send, kb_recv),
        ("kw", "b", "prev"): Gather(p, "b", kwb.at[0], kp_send, kp_recv),
    }
    barrier = pltpu.get_barrier_semaphore()
    x_ways = [("x", s) for s in (1, -1, 2)]
    z_ways = [("z", s) for s in (1, -1, 2, -2, 3, -3, 4)]
    for way in x_ways + z_ways:
        pl.semaphore_signal(barrier, inc=1, device_id=p.toward(way), device_id_type=MESH)
    pl.semaphore_signal(barrier, inc=1, device_id={"cont": p.behind}, device_id_type=MESH)

    arrays = (
        (sv_hbm, sv), (xy_hbm, xy), (cells_hbm, cells), (cond_hbm, cond), (tiles_hbm, tiles),
        (weights_hbm, weights), (factor_hbm, factor),
    )
    loads = [pltpu.make_async_copy(*pair, in_sem.at[i]) for i, pair in enumerate(arrays)]
    for load in loads:
        load.start()
    rain_copy = pltpu.make_async_copy(rain, rain_raw, rain_sem)
    rain_copy.start()
    loads[0].wait()
    loads[1].wait()
    sva[slot_a] = sv[0, :SV_A, :]
    svb[slot_b] = jnp.concatenate(
        [sv[0, SV_A:, :], jnp.zeros((ROWS - DAYS, BS), BF16)], axis=0
    )
    row_coords[p.x] = jnp.concatenate(
        [xy[0].astype(F32) * SCALE, jnp.zeros((6, BS), F32)], axis=0
    )
    pl.semaphore_wait(barrier, XS + ZS - 1)

    own = row_coords.at[p.x]
    for i, way in enumerate(x_ways):
        remote(own, own, c_send, c_recv.at[i], p.toward(way)).start()

    def coords_x():
        for i, (_, s) in enumerate(x_ways):
            ref = row_coords.at[p.xs[2 if s == 2 else -s]]
            remote(ref, ref, c_send, c_recv.at[i], here).wait_recv()
        coords[1, p.z] = jnp.concatenate([row_coords[x, 0:2, :] for x in range(XS)], axis=0)
        ref = coords.at[1, p.z]
        for i, way in enumerate(z_ways):
            remote(ref, ref, cz_send, c_recv.at[3 + i], p.toward(way)).start()

    coord_ahead = remote(coords.at[1], coords.at[0], cc_send, c_recv.at[10], {"cont": p.ahead})

    def coords_z():
        for i, (_, s) in enumerate(z_ways):
            ref = coords.at[1, p.zs[4 if s == 4 else -s]]
            remote(ref, ref, cz_send, c_recv.at[3 + i], here).wait_recv()
        coord_ahead.start()

    def place_cells(first, last):
        def one(c, carry):
            lanes = pl.ds(pl.multiple_of(c * 128, 128), 128)
            for row, held in ((0, cellx), (1, celly)):
                line = cells[row : row + 1, lanes] * SCALE
                held[lanes, :] = jnp.transpose(jnp.broadcast_to(line, (128, 128)))
            return carry

        lax.fori_loop(first, last, one, 0)

    def place_rain():
        rain_copy.wait()
        rain_win[...] = jnp.zeros_like(rain_win)
        rain_win[WOFF : WOFF + WIN, :] = rain_raw[...]

    def listed(t, k):
        block = tiles[t, k]
        own = jnp.where(block // GROUP == p.cont, 1, 0)
        dev = block % GROUP
        return own, dev % ZS * XS + dev // ZS, dev

    def cover(first, last):
        def one(g, carry):
            t, k = g // LISTED, g % LISTED
            own, _, dev = listed(t, k)
            x, z = dev // ZS, dev % ZS
            sx, sy = coords[own, z, pl.ds(2 * x, 1), :], coords[own, z, pl.ds(2 * x + 1, 1), :]
            lanes = pl.ds(pl.multiple_of(k * BS, BS), BS)

            def part(c, carry):
                rows = pl.ds(pl.multiple_of(t * TILE + c * 256, 256), 256)
                dx = cellx[rows, :] - sx
                dy = celly[rows, :] - sy
                square = dx * dx + dy * dy + NUGGET
                cov[rows, lanes] = jnp.exp2(-4.0 - square * lax.rsqrt(square)).astype(BF16)
                return carry

            return lax.fori_loop(0, TILE // 256, part, carry)

        lax.fori_loop(first, last, one, 0)

    def krige(kind):
        first, last = (0, KW_A) if kind == "a" else (KW_A, ROWS)

        def days(dev):
            below = sva[dev % ZS * XS + dev // ZS, first:SV_A, :] if first < SV_A else None
            above = svb[dev, max(first - SV_A, 0) : last - SV_A, :]
            return above if below is None else jnp.concatenate([below, above], axis=0)

        rows = pl.ds(first, last - first)
        for k in range(NCOND):
            prior[rows, k * BS : (k + 1) * BS] = days(cond[0, k] % GROUP)
        predicted = dot(prior[rows, :], weights[0], ((1,), (1,)))
        innovation = (days(p.dev).astype(F32) - predicted).astype(BF16)
        whitened = dot(innovation, factor[0], ((1,), (1,))).astype(BF16)
        kweights = dot(whitened, factor[0]).astype(BF16)
        if kind == "a":
            kwa[1, slot_a] = kweights
        else:
            kwb[1, slot_b] = kweights

            @pl.when(odd)
            def _():
                remote(
                    kwb.at[1, slot_b], kwb.at[0, slot_b], inj_send, inj_recv, {"cont": p.ahead}
                ).start()

    def lend(kind, item):
        buf, send, recv = (kwa, fa_send, fa_recv) if kind == "a" else (kwb, fb_send, fb_recv)
        x, z = p.xs[item[0]], p.zs[item[1]]
        part = pl.ds(z * XS, XS) if kind == "a" else pl.ds(x * ZS, ZS)
        remote(buf.at[1, part], buf.at[0, part], send, recv, {"cont": p.ahead}).start()

    def act(step):
        what, stage, kind, source, item = step[:5]
        if what == "send":
            gathers[stage, kind, source].send_on(item, step[6])
        elif what == "lend" and kind == "a":
            lend(kind, item)
        elif what == "lend":
            pl.when(p.even)(lambda: lend(kind, item))
        elif source == "prev" and item == (0, 0, 0):
            ref = kwb.at[0, slot_b]
            remote(ref, ref, inj_send, inj_recv, here).wait_recv()
        else:
            gathers[stage, kind, source].arrive(item)

    def finish_loads():
        for load in loads[2:]:
            load.wait()

    early = [
        (1.0, finish_loads),
        (1.0, lambda: place_cells(0, 8)),
        (3.4, coords_x),
        (4.0, lambda: place_cells(8, 16)),
        (7.0, lambda: place_cells(16, 24)),
        (9.0, coords_z),
        (9.0, lambda: place_cells(24, CELLS // 128)),
        (READY - 1.0, place_rain),
        (READY - 1.0, coord_ahead.wait_recv),
    ]
    done = 0
    steps = schedule()
    while steps:
        step = steps.pop(0)
        if step[0] == "cover":
            cover(done, done + step[1])
            done += step[1]
        elif step[0] == "krige":
            krige(step[1])
        else:
            while early and early[0][0] < step[5]:
                early.pop(0)[1]()
            batch = [step]
            if step[3] == "prev":
                while steps and len(steps[0]) > 2 and steps[0][3] == "prev":
                    batch.append(steps.pop(0))

                @pl.when(p.even)
                def _(batch=batch):
                    for one in batch:
                        act(one)
            else:
                act(step)

    whole = kwa.at[0]
    remote(whole, whole, fa_send, fa_recv, here).wait_recv()

    @pl.when(odd)
    def _():
        ref = kwb.at[0]
        remote(ref, ref, fb_send, fb_recv, here).wait_recv()

    def choose(t, chosen):
        for k in range(LISTED):
            own, at, dev = listed(t, k)
            chosen[:KW_A, k * BS : (k + 1) * BS] = kwa[own, at]
            chosen[KW_A:, k * BS : (k + 1) * BS] = kwb[own, dev]

    def tile(t, chosen):
        at = pl.ds(pl.multiple_of(t * TILE, TILE), TILE)
        full = dot(chosen[...], cov[at, :], ((1,), (1,)))
        out[:, at] = full[:DAYS].astype(BF16)
        soft = jnp.tanh((rain_win[:, at] - full[WROW : WROW + WROWS]) * 2.0)
        row = lax.broadcasted_iota(jnp.int32, soft.shape, 0)
        soft = jnp.where((row >= WOFF) & (row < WOFF + WIN), soft, 0.0)
        total = jnp.sum(soft, axis=0, keepdims=True)
        share[:, at] = total * (0.5 / WIN) + 0.5

    def two_tiles(i, carry):
        choose(2 * i + 1, chosen_b)
        tile(2 * i, chosen_a)
        choose(jnp.minimum(2 * i + 2, TILES - 1), chosen_a)
        tile(2 * i + 1, chosen_b)
        return carry

    choose(0, chosen_a)
    lax.fori_loop(0, TILES // 2, two_tiles, 0)

    for (_, _, source), gather in gathers.items():
        if source == "own":
            gather.sent()
    ref = row_coords.at[pl.ds(0, XS - 1)]
    remote(ref, ref, c_send, c_recv.at[0], here).wait_send()
    ref = coords.at[1, pl.ds(0, ZS - 1)]
    remote(ref, ref, cz_send, c_recv.at[0], here).wait_send()
    coord_ahead.wait_send()
    remote(whole, whole, fa_send, fa_recv, here).wait_send()

    @pl.when(odd)
    def _():
        remote(
            kwb.at[1, slot_b], kwb.at[0, slot_b], inj_send, inj_recv, {"cont": p.ahead}
        ).wait_send()

    @pl.when(p.even)
    def _():
        gathers["kw", "b", "prev"].sent()
        ref = kwb.at[1]
        remote(ref, ref, fb_send, fb_recv, here).wait_send()


def per_device(sv, weights, factor, cond, xy, cells, tiles, rain):
    dma = pltpu.SemaphoreType.DMA
    vmem, hbm = pl.BlockSpec(memory_space=pltpu.VMEM), pl.BlockSpec(memory_space=pltpu.HBM)
    inputs = (cond, tiles, jnp.swapaxes(sv, 1, 2), weights, factor, xy, cells, rain)
    inputs = [pltpu.with_memory_space_constraint(a, pltpu.HBM) for a in inputs]
    thresholds, share = pl.pallas_call(
        kernel,
        out_shape=(
            jax.ShapeDtypeStruct((DAYS, CELLS), BF16),
            jax.ShapeDtypeStruct((1, CELLS), F32),
        ),
        in_specs=[hbm] * len(inputs),
        out_specs=(vmem, vmem),
        scratch_shapes=[
            pltpu.SMEM(cond.shape, jnp.int32),
            pltpu.SMEM(tiles.shape, jnp.int32),
            *(pltpu.VMEM(a.shape, a.dtype) for a in inputs[2:7]),
            dma((7,)),
            pltpu.VMEM((GROUP, SV_A, BS), BF16),
            pltpu.VMEM((GROUP, ROWS - SV_A, BS), BF16),
            pltpu.VMEM((2, GROUP, KW_A, BS), BF16),
            pltpu.VMEM((2, GROUP, ROWS - KW_A, BS), BF16),
            pltpu.VMEM((XS, 8, BS), F32),
            pltpu.VMEM((2, ZS, 2 * XS, BS), F32),
            pltpu.VMEM((CELLS, 128), F32),
            pltpu.VMEM((CELLS, 128), F32),
            pltpu.VMEM((WIN, CELLS), F32),
            pltpu.VMEM((WROWS, CELLS), F32),
            pltpu.VMEM((ROWS, NCOND * BS), BF16),
            pltpu.VMEM((CELLS, STATIONS), BF16),
            pltpu.VMEM((ROWS, STATIONS), BF16),
            pltpu.VMEM((ROWS, STATIONS), BF16),
            dma,
            dma, dma((XS + ZS - 1,)), dma, dma,
            dma, dma((len(ITEMS["a"]),)), dma, dma((len(ITEMS["b"]),)),
            dma, dma((len(ITEMS["a"]),)), dma, dma((len(ITEMS["b"]),)), dma, dma((len(ITEMS["b"]),)),
            dma, dma, dma, dma, dma, dma,
        ],
        compiler_params=pltpu.CompilerParams(
            collective_id=0, has_side_effects=True, vmem_limit_bytes=44 * 1024 * 1024
        ),
    )(*inputs)
    return thresholds.T, share.reshape(-1)


def solution(mesh):
    both = ("cont", "dev")
    placed = (
        P(both, None, None),
        P(both, None, None),
        P(both, None, None),
        P(both, None),
        P(both, None, None),
        P(None, both),
        P(both, None),
        P(None, both),
    )
    return jax.shard_map(
        per_device,
        mesh=mesh,
        in_specs=placed,
        out_specs=(P(both, None), P(both)),
        check_vma=False,
    )
```

```python
import heapq
import math

import jax
import jax.numpy as jnp
from jax import lax
from jax.experimental import pallas as pl
from jax.experimental.pallas import tpu as pltpu
from jax.sharding import PartitionSpec as P

MESH = pl.DeviceIdType.MESH
BF16 = jnp.bfloat16
F32 = jnp.float32

XS, ZS = 4, 8
GROUP = XS * ZS
CONTS = 8
BS = 128
DAYS = 366
ROWS = 368
SV_A, KW_A = 176, 192
NCOND = 4
LISTED = 16
STATIONS = LISTED * BS
TILES = 4
TILE = 1024
CELLS = TILES * TILE
WIN = 60
WSTART = 150
WROW = WSTART // 8 * 8
WOFF = WSTART - WROW
WROWS = -(-(WOFF + WIN) // 8) * 8
LENGTH = 9.0 * STATIONS**-0.5
SCALE = math.log2(math.e) / LENGTH
NUGGET = (LENGTH * 0.1 * SCALE) ** 2


class Place:
    def __init__(self):
        self.dev, self.cont = lax.axis_index("dev"), lax.axis_index("cont")
        self.x, self.z = self.dev // ZS, self.dev % ZS
        self.xs = {s: lax.rem(self.x + (s + XS), XS) for s in (-1, 0, 1, 2)}
        self.zs = {s: lax.rem(self.z + (s + ZS), ZS) for s in (-3, -2, -1, 0, 1, 2, 3, 4)}
        self.ahead = lax.rem(self.cont + 1, CONTS)
        self.behind = lax.rem(self.cont + CONTS - 1, CONTS)
        self.even = lax.rem(self.cont, 2) == 0

    def toward(self, way):
        axis, step = way
        if axis == "cont":
            return {"cont": self.ahead}
        x, z = (self.xs[step], self.z) if axis == "x" else (self.x, self.zs[step])
        return {"dev": x * ZS + z}


def remote(src, dst, send, recv, device):
    return pltpu.make_async_remote_copy(
        src_ref=src, dst_ref=dst, send_sem=send, recv_sem=recv, device_id=device, device_id_type=MESH
    )


def along_x_first(item):
    dx, dz, part = item
    sends = []
    if dz == 0:
        if dx == 0:
            sends += [(("x", s), (-s, 0, 0)) for s in (1, -1)] + [(("x", 2), (2, 0, 0))]
        sends += [(("z", s), (dx, -s, 0)) for s in (1, -1)]
    elif abs(dz) < 3 or (abs(dz) == 3 and (dz < 0) == (dx in (0, 1))):
        step = 1 if dz < 0 else -1
        far = dz - step
        sends.append((("z", step), (dx, 4 if abs(far) == 4 else far, 0)))
    return sends


def along_z_first(item):
    dx, dz, part = item
    sends = []
    if dx == 0:
        if dz == 0:
            sends += [(("z", s), (0, -s, 0)) for s in (1, -1)]
        elif abs(dz) < 3:
            step = 1 if dz < 0 else -1
            sends.append((("z", step), (0, dz - step, 0)))
        elif abs(dz) == 3:
            step = 1 if dz < 0 else -1
            sends.append((("z", step), (0, 4, step)))
        sends += [(("x", s), (-s, dz, 0)) for s in (1, -1)]
        if dz == 4:
            sends.append((("x", 2), (2, 4, 0)))
    elif dx != 2 and dz != 4:
        if dz == 0:
            sends.append((("x", -dx), (2, 0, dx)))
        elif (dz < 0) == (dx < 0):
            sends.append((("x", -dx), (2, dz, 0)))
    return sends


def items_of(sends_of):
    found, todo = [], [(0, 0, 0)]
    while todo:
        item = todo.pop(0)
        found.append(item)
        if item[2] == 0:
            todo += [arrival for _, arrival in sends_of(item)]
        elif (*item[:2], 0) not in found:
            todo.append((*item[:2], 0))
            found.append((*item[:2], 0))
            todo.pop()
            todo += [arrival for _, arrival in sends_of((*item[:2], 0))]
    return list(dict.fromkeys(found))


SENDS = {"a": along_x_first, "b": along_z_first}
ITEMS = {kind: items_of(sends) for kind, sends in SENDS.items()}
SEM = {kind: {item: i for i, item in enumerate(items)} for kind, items in ITEMS.items()}
HALF_ROWS = {"sv": {"a": SV_A, "b": ROWS - SV_A}, "kw": {"a": KW_A, "b": ROWS - KW_A}}


class Gather:
    def __init__(self, place, kind, buf, send, recv):
        self.place, self.kind, self.buf, self.send, self.recv = place, kind, buf, send, recv
        self.rows = buf.shape[1]

    def ref(self, item):
        dx, dz, part = item
        x, z = self.place.xs[dx], self.place.zs[dz]
        slot = z * XS + x if self.kind == "a" else x * ZS + z
        if part == 0:
            return self.buf.at[slot]
        cut = self.rows // 32 * 16
        first, last = (0, cut) if part < 0 else (cut, self.rows)
        return self.buf.at[slot, pl.ds(first, last - first)]

    def send_on(self, item, index):
        way, arrival = SENDS[self.kind](item)[index]
        ref = self.ref((*item[:2], arrival[2]))
        sem = self.recv.at[SEM[self.kind][arrival]]
        remote(ref, ref, self.send, sem, self.place.toward(way)).start()

    def arrive(self, item):
        ref = self.ref(item)
        sem = self.recv.at[SEM[self.kind][item]]
        remote(ref, ref, self.send, sem, {"dev": self.place.dev}).wait_recv()

    def sent(self):
        ref = self.buf.at[pl.ds(0, GROUP - 1)]
        remote(ref, ref, self.send, self.recv.at[0], {"dev": self.place.dev}).wait_send()


RATE, HOP, MORE, CORE_RATE, CORE_HOP, ISSUE = 92e3, 3.2, 0.62, 1.4e6, 0.75, 0.08
KRIGING = 0.8
STEP_COST = 0.28
READY = 14.0


LEND = {"a": XS, "b": ZS}
DEPTH = 1.0


def chain(kind, item):
    return max([1 + chain(kind, (*to[:2], 0)) for _, to in SENDS[kind](item)], default=0)


def schedule():
    links, queue, clock = {}, [], [0.0, 0.0]
    plan, whole, got, lent, count = [], {}, {}, {}, 0
    left = [TILES * LISTED] * 2
    waiting = ([], [])

    def post(core, way, size, target, arrival):
        nonlocal count
        clock[core] += ISSUE
        end = clock[core]
        if way == ("cont", 0):
            end += size / CORE_RATE + CORE_HOP
        else:
            lanes = [(way[0], 1), (way[0], -1)] if way[1] == 2 else [way]
            for lane in lanes:
                links[lane] = max(clock[core], links.get(lane, 0.0)) + size / RATE
                end = max(end, links[lane])
            end += HOP + (MORE if way[1] == 2 else 0.0)
        count += 1
        heapq.heappush(queue, (end, count, target, arrival))

    def flush(core):
        later = []
        soon = queue[0][0] if queue else 1e9
        for entry in sorted(waiting[core]):
            _, _, index, stage, kind, source, item = entry
            way, arrival = SENDS[kind](item)[index]
            lanes = [(way[0], 1), (way[0], -1)] if way[1] == 2 else [way]
            free = min(links.get(lane, 0.0) for lane in lanes)
            if free > max(clock[core] + DEPTH, soon):
                later.append(entry)
                continue
            size = HALF_ROWS[stage][kind] * BS * 2
            post(core, way, size if arrival[2] == 0 else size / 2, core, (stage, kind, source, arrival))
            if core == 0:
                plan.append(("send", stage, kind, source, item, clock[0], index))
        waiting[core][:] = later

    def forward(core, stage, kind, source, item):
        nonlocal count
        size = HALF_ROWS[stage][kind] * BS * 2
        if kind == "b" and core == 1 and stage == "kw" and item == (0, 0, 0):
            post(1, ("y", 1), size, 0, (stage, kind, "prev", item))
        if source == "own" or (kind == "b" and core == 0):
            for index, (way, arrival) in enumerate(SENDS[kind](item)):
                count += 1
                ahead = chain(kind, (*arrival[:2], 0))
                waiting[core].append((-ahead, count, index, stage, kind, source, item))
        if source == "own" and stage == "kw" and (kind == "a" or core == 0):
            group = item[1] if kind == "a" else item[0]
            size *= LEND[kind]
            have = lent[core, kind, group] = lent.get((core, kind, group), 0) + 1
            if have % LEND[kind]:
                return
            way = ("cont", 0) if core == 0 else ("y", 1)
            post(core, way, size, 1 - core, (stage, kind, "prev", item))
            if core == 0:
                plan.append(("lend", stage, kind, source, item, clock[0]))

    for kind in ("b", "a"):
        for core in (0, 1):
            forward(core, "sv", kind, "own", (0, 0, 0))
    while queue or waiting[0] or waiting[1]:
        for core in (0, 1):
            flush(core)
        if not queue:
            continue
        when, _, core, (stage, kind, source, item) = heapq.heappop(queue)
        passive = source == "prev" and (kind == "a" or core == 1)
        if passive:
            continue
        while left[core] and when - max(clock[core], READY) > STEP_COST / 4:
            clock[core] = max(clock[core], READY) + STEP_COST
            left[core] -= 1
            if core == 0 and plan[-1][0] == "cover":
                plan[-1] = ("cover", plan[-1][1] + 1)
            elif core == 0:
                plan.append(("cover", 1))
            flush(core)
        clock[core] = max(clock[core], when) + ISSUE
        if core == 0:
            plan.append(("arrive", stage, kind, source, item, clock[0]))
        if item[2]:
            item = (*item[:2], 0)
            key = (core, stage, kind, source, item)
            whole[key] = whole.get(key, 0) + 1
            if whole[key] < 2:
                continue
        forward(core, stage, kind, source, item)
        if stage == "sv":
            got[core, kind] = got.get((core, kind), 1) + 1
            ready = []
            if kind == "b" and got[core, "b"] == GROUP:
                ready.append("b")
            if got.get((core, "a")) == got.get((core, "b")) == GROUP:
                ready.append("a")
            for half in ready:
                clock[core] += KRIGING
                if core == 0:
                    plan.append(("krige", half))
                forward(core, "kw", half, "own", (0, 0, 0))
    plan.append(("cover", left[0]))
    return plan


def dot(a, b, dims=((1,), (0,))):
    return lax.dot_general(a, b, (dims, ((), ())), preferred_element_type=F32)


def listing(tiles, cont, t, k):
    block = tiles[t, k]
    own = jnp.where(block // GROUP == cont, 1, 0)
    dev = block % GROUP
    return own, dev % ZS * XS + dev // ZS, dev


def kernel(
    cond_hbm, tiles_hbm, sv_hbm, weights_hbm, factor_hbm, xy_hbm, cells_hbm, rain,
    kwa, kwb, cov, rain_win, tiles_kept,
    cond, tiles, sv, weights, factor, xy, cells, in_sem,
    sva, svb, row_coords, coords, cellx, celly, rain_raw, prior,
    rain_sem,
    c_send, c_recv, cz_send, cc_send,
    sa_send, sa_recv, sb_send, sb_recv,
    ka_send, ka_recv, kb_send, kb_recv, kp_send, kp_recv,
    fa_send, fa_recv, fb_send, fb_recv, inj_send, inj_recv,
):
    p = Place()
    odd = jnp.logical_not(p.even)
    slot_a, slot_b = p.z * XS + p.x, p.dev
    here = {"dev": p.dev}
    gathers = {
        ("sv", "a", "own"): Gather(p, "a", sva, sa_send, sa_recv),
        ("sv", "b", "own"): Gather(p, "b", svb, sb_send, sb_recv),
        ("kw", "a", "own"): Gather(p, "a", kwa.at[1], ka_send, ka_recv),
        ("kw", "b", "own"): Gather(p, "b", kwb.at[1], kb_send, kb_recv),
        ("kw", "b", "prev"): Gather(p, "b", kwb.at[0], kp_send, kp_recv),
    }
    barrier = pltpu.get_barrier_semaphore()
    x_ways = [("x", s) for s in (1, -1, 2)]
    z_ways = [("z", s) for s in (1, -1, 2, -2, 3, -3, 4)]
    for way in x_ways + z_ways:
        pl.semaphore_signal(barrier, inc=1, device_id=p.toward(way), device_id_type=MESH)
    pl.semaphore_signal(barrier, inc=1, device_id={"cont": p.behind}, device_id_type=MESH)

    arrays = (
        (sv_hbm, sv), (xy_hbm, xy), (cells_hbm, cells), (cond_hbm, cond), (tiles_hbm, tiles),
        (weights_hbm, weights), (factor_hbm, factor), (tiles_hbm, tiles_kept),
    )
    loads = [pltpu.make_async_copy(*pair, in_sem.at[i]) for i, pair in enumerate(arrays)]
    for load in loads:
        load.start()
    rain_copy = pltpu.make_async_copy(rain, rain_raw, rain_sem)
    rain_copy.start()
    loads[0].wait()
    loads[1].wait()
    sva[slot_a] = sv[0, :SV_A, :]
    svb[slot_b] = jnp.concatenate(
        [sv[0, SV_A:, :], jnp.zeros((ROWS - DAYS, BS), BF16)], axis=0
    )
    row_coords[p.x] = jnp.concatenate(
        [xy[0].astype(F32) * SCALE, jnp.zeros((6, BS), F32)], axis=0
    )
    pl.semaphore_wait(barrier, XS + ZS - 1)

    own = row_coords.at[p.x]
    for i, way in enumerate(x_ways):
        remote(own, own, c_send, c_recv.at[i], p.toward(way)).start()

    def coords_x():
        for i, (_, s) in enumerate(x_ways):
            ref = row_coords.at[p.xs[2 if s == 2 else -s]]
            remote(ref, ref, c_send, c_recv.at[i], here).wait_recv()
        coords[1, p.z] = jnp.concatenate([row_coords[x, 0:2, :] for x in range(XS)], axis=0)
        ref = coords.at[1, p.z]
        for i, way in enumerate(z_ways):
            remote(ref, ref, cz_send, c_recv.at[3 + i], p.toward(way)).start()

    coord_ahead = remote(coords.at[1], coords.at[0], cc_send, c_recv.at[10], {"cont": p.ahead})

    def coords_z():
        for i, (_, s) in enumerate(z_ways):
            ref = coords.at[1, p.zs[4 if s == 4 else -s]]
            remote(ref, ref, cz_send, c_recv.at[3 + i], here).wait_recv()
        coord_ahead.start()

    def place_cells(first, last):
        def one(c, carry):
            lanes = pl.ds(pl.multiple_of(c * 128, 128), 128)
            for row, held in ((0, cellx), (1, celly)):
                line = cells[row : row + 1, lanes] * SCALE
                held[lanes, :] = jnp.transpose(jnp.broadcast_to(line, (128, 128)))
            return carry

        lax.fori_loop(first, last, one, 0)

    def place_rain():
        rain_copy.wait()
        rain_win[...] = jnp.zeros_like(rain_win)
        rain_win[WOFF : WOFF + WIN, :] = rain_raw[...]

    def listed(t, k):
        return listing(tiles, p.cont, t, k)

    def cover(first, last):
        def one(g, carry):
            t, k = g // LISTED, g % LISTED
            own, _, dev = listed(t, k)
            x, z = dev // ZS, dev % ZS
            sx, sy = coords[own, z, pl.ds(2 * x, 1), :], coords[own, z, pl.ds(2 * x + 1, 1), :]
            lanes = pl.ds(pl.multiple_of(k * BS, BS), BS)

            def part(c, carry):
                rows = pl.ds(pl.multiple_of(t * TILE + c * 256, 256), 256)
                dx = cellx[rows, :] - sx
                dy = celly[rows, :] - sy
                square = dx * dx + dy * dy + NUGGET
                cov[rows, lanes] = jnp.exp2(-4.0 - square * lax.rsqrt(square)).astype(BF16)
                return carry

            return lax.fori_loop(0, TILE // 256, part, carry)

        lax.fori_loop(first, last, one, 0)

    def krige(kind):
        first, last = (0, KW_A) if kind == "a" else (KW_A, ROWS)

        def days(dev):
            below = sva[dev % ZS * XS + dev // ZS, first:SV_A, :] if first < SV_A else None
            above = svb[dev, max(first - SV_A, 0) : last - SV_A, :]
            return above if below is None else jnp.concatenate([below, above], axis=0)

        rows = pl.ds(first, last - first)
        for k in range(NCOND):
            prior[rows, k * BS : (k + 1) * BS] = days(cond[0, k] % GROUP)
        predicted = dot(prior[rows, :], weights[0], ((1,), (1,)))
        innovation = (days(p.dev).astype(F32) - predicted).astype(BF16)
        whitened = dot(innovation, factor[0], ((1,), (1,))).astype(BF16)
        kweights = dot(whitened, factor[0]).astype(BF16)
        if kind == "a":
            kwa[1, slot_a] = kweights
        else:
            kwb[1, slot_b] = kweights

            @pl.when(odd)
            def _():
                remote(
                    kwb.at[1, slot_b], kwb.at[0, slot_b], inj_send, inj_recv, {"cont": p.ahead}
                ).start()

    def lend(kind, item):
        buf, send, recv = (kwa, fa_send, fa_recv) if kind == "a" else (kwb, fb_send, fb_recv)
        x, z = p.xs[item[0]], p.zs[item[1]]
        part = pl.ds(z * XS, XS) if kind == "a" else pl.ds(x * ZS, ZS)
        remote(buf.at[1, part], buf.at[0, part], send, recv, {"cont": p.ahead}).start()

    def act(step):
        what, stage, kind, source, item = step[:5]
        if what == "send":
            gathers[stage, kind, source].send_on(item, step[6])
        elif what == "lend" and kind == "a":
            lend(kind, item)
        elif what == "lend":
            pl.when(p.even)(lambda: lend(kind, item))
        elif source == "prev" and item == (0, 0, 0):
            ref = kwb.at[0, slot_b]
            remote(ref, ref, inj_send, inj_recv, here).wait_recv()
        else:
            gathers[stage, kind, source].arrive(item)

    def finish_loads():
        for load in loads[2:]:
            load.wait()

    early = [
        (1.0, finish_loads),
        (1.0, lambda: place_cells(0, 8)),
        (3.4, coords_x),
        (4.0, lambda: place_cells(8, 16)),
        (7.0, lambda: place_cells(16, 24)),
        (9.0, coords_z),
        (9.0, lambda: place_cells(24, CELLS // 128)),
        (READY - 1.0, place_rain),
        (READY - 1.0, coord_ahead.wait_recv),
    ]
    done = 0
    steps = schedule()
    while steps:
        step = steps.pop(0)
        if step[0] == "cover":
            cover(done, done + step[1])
            done += step[1]
        elif step[0] == "krige":
            krige(step[1])
        else:
            while early and early[0][0] < step[5]:
                early.pop(0)[1]()
            batch = [step]
            if step[3] == "prev":
                while steps and len(steps[0]) > 2 and steps[0][3] == "prev":
                    batch.append(steps.pop(0))

                @pl.when(p.even)
                def _(batch=batch):
                    for one in batch:
                        act(one)
            else:
                act(step)

    whole = kwa.at[0]
    remote(whole, whole, fa_send, fa_recv, here).wait_recv()

    @pl.when(odd)
    def _():
        ref = kwb.at[0]
        remote(ref, ref, fb_send, fb_recv, here).wait_recv()

    for (_, _, source), gather in gathers.items():
        if source == "own":
            gather.sent()
    ref = row_coords.at[pl.ds(0, XS - 1)]
    remote(ref, ref, c_send, c_recv.at[0], here).wait_send()
    ref = coords.at[1, pl.ds(0, ZS - 1)]
    remote(ref, ref, cz_send, c_recv.at[0], here).wait_send()
    coord_ahead.wait_send()
    remote(whole, whole, fa_send, fa_recv, here).wait_send()

    @pl.when(odd)
    def _():
        remote(
            kwb.at[1, slot_b], kwb.at[0, slot_b], inj_send, inj_recv, {"cont": p.ahead}
        ).wait_send()

    @pl.when(p.even)
    def _():
        gathers["kw", "b", "prev"].sent()
        ref = kwb.at[1]
        remote(ref, ref, fb_send, fb_recv, here).wait_send()


def interpolate(
    kwa, kwb, cov, rain_win, tiles_kept, out, share, chosen_a, chosen_b, stage, out_sem, tiles, sem
):
    load = pltpu.make_async_copy(tiles_kept, tiles, sem)
    load.start()
    load.wait()
    cont = lax.axis_index("cont")

    def listed(t, k):
        return listing(tiles, cont, t, k)

    def choose(t, chosen):
        for k in range(LISTED):
            own, at, dev = listed(t, k)
            chosen[:KW_A, k * BS : (k + 1) * BS] = kwa[own, at]
            chosen[KW_A:, k * BS : (k + 1) * BS] = kwb[own, dev]

    def copy_out(t, slot):
        at = pl.ds(pl.multiple_of(t * TILE, TILE), TILE)
        return pltpu.make_async_copy(stage.at[slot], out.at[:, at], out_sem.at[slot])

    def tile(t, chosen, slot):
        at = pl.ds(pl.multiple_of(t * TILE, TILE), TILE)
        full = dot(chosen[...], cov[at, :], ((1,), (1,)))
        held = stage.at[slot]
        held[...] = full[:DAYS].astype(BF16)
        copy_out(t, slot).start()
        soft = jnp.tanh((rain_win[:, at] - full[WROW : WROW + WROWS]) * 2.0)
        row = lax.broadcasted_iota(jnp.int32, soft.shape, 0)
        soft = jnp.where((row >= WOFF) & (row < WOFF + WIN), soft, 0.0)
        total = jnp.sum(soft, axis=0, keepdims=True)
        share[at] = (total * (0.5 / WIN) + 0.5)[0]

    def two_tiles(i, carry):
        choose(2 * i + 1, chosen_b)
        tile(2 * i, chosen_a, 2 * i)
        choose(jnp.minimum(2 * i + 2, TILES - 1), chosen_a)
        tile(2 * i + 1, chosen_b, 2 * i + 1)
        return carry

    choose(0, chosen_a)
    lax.fori_loop(0, TILES // 2, two_tiles, 0)
    for t in range(TILES):
        copy_out(t, t).wait()


def per_device(sv, weights, factor, cond, xy, cells, tiles, rain):
    dma = pltpu.SemaphoreType.DMA
    vmem, hbm = pl.BlockSpec(memory_space=pltpu.VMEM), pl.BlockSpec(memory_space=pltpu.HBM)
    inputs = (cond, tiles, jnp.swapaxes(sv, 1, 2), weights, factor, xy, cells, rain)
    inputs = [pltpu.with_memory_space_constraint(a, pltpu.HBM) for a in inputs]
    found = pl.pallas_call(
        kernel,
        out_shape=(
            jax.ShapeDtypeStruct((2, GROUP, KW_A, BS), BF16),
            jax.ShapeDtypeStruct((2, GROUP, ROWS - KW_A, BS), BF16),
            jax.ShapeDtypeStruct((CELLS, STATIONS), BF16),
            jax.ShapeDtypeStruct((WROWS, CELLS), F32),
            jax.ShapeDtypeStruct(tiles.shape, jnp.int32),
        ),
        in_specs=[hbm] * len(inputs),
        out_specs=(vmem,) * 5,
        scratch_shapes=[
            pltpu.SMEM(cond.shape, jnp.int32),
            pltpu.SMEM(tiles.shape, jnp.int32),
            *(pltpu.VMEM(a.shape, a.dtype) for a in inputs[2:7]),
            dma((8,)),
            pltpu.VMEM((GROUP, SV_A, BS), BF16),
            pltpu.VMEM((GROUP, ROWS - SV_A, BS), BF16),
            pltpu.VMEM((XS, 8, BS), F32),
            pltpu.VMEM((2, ZS, 2 * XS, BS), F32),
            pltpu.VMEM((CELLS, 128), F32),
            pltpu.VMEM((CELLS, 128), F32),
            pltpu.VMEM((WIN, CELLS), F32),
            pltpu.VMEM((ROWS, NCOND * BS), BF16),
            dma,
            dma, dma((XS + ZS - 1,)), dma, dma,
            dma, dma((len(ITEMS["a"]),)), dma, dma((len(ITEMS["b"]),)),
            dma, dma((len(ITEMS["a"]),)), dma, dma((len(ITEMS["b"]),)), dma, dma((len(ITEMS["b"]),)),
            dma, dma, dma, dma, dma, dma,
        ],
        compiler_params=pltpu.CompilerParams(
            collective_id=0, has_side_effects=True, vmem_limit_bytes=14 * 1024 * 1024
        ),
    )(*inputs)
    found = [pltpu.with_memory_space_constraint(a, pltpu.VMEM) for a in found]
    thresholds, share = pl.pallas_call(
        interpolate,
        out_shape=(
            jax.ShapeDtypeStruct((DAYS, CELLS), BF16),
            jax.ShapeDtypeStruct((CELLS,), F32),
        ),
        in_specs=[vmem] * len(found),
        out_specs=(hbm, vmem),
        scratch_shapes=[
            pltpu.VMEM((ROWS, STATIONS), BF16),
            pltpu.VMEM((ROWS, STATIONS), BF16),
            pltpu.VMEM((TILES, DAYS, TILE), BF16),
            dma((TILES,)),
            pltpu.SMEM(tiles.shape, jnp.int32),
            dma,
        ],
        compiler_params=pltpu.CompilerParams(vmem_limit_bytes=16 * 1024 * 1024),
    )(*found)
    return thresholds.T, share


def solution(mesh):
    both = ("cont", "dev")
    placed = (
        P(both, None, None),
        P(both, None, None),
        P(both, None, None),
        P(both, None),
        P(both, None, None),
        P(None, both),
        P(both, None),
        P(None, both),
    )
    return jax.shard_map(
        per_device,
        mesh=mesh,
        in_specs=placed,
        out_specs=(P(both, None), P(both)),
        check_vma=False,
    )
```
